32 devices in a mesh: dp: 4 (over z), ctx: 8 (over y, x, core).
Axes of the slice: x: 2, y: 2, z: 4, core: 2. Of those that a mesh axis runs over, the one named last changes fastest.
Arguments:
- tokens: bfloat16 [8, 1024, 768], P('dp', 'ctx'), may hold values from -6 to 6
- attn_qkv: bfloat16 [3, 768, 768], P(None, ('dp', 'ctx')), may hold values from -0.21875 to 0.21875
- attn_out: bfloat16 [768, 768], P(('dp', 'ctx')), may hold values from -1.75 to 1.75
- norm_gains: bfloat16 [2, 768], P(None, ('dp', 'ctx')), may hold values from 0.5 to 1.5
- router: bfloat16 [768, 8], P(('dp', 'ctx')), may hold values from -0.109375 to 0.109375
- rel_table: bfloat16 [384], P(('dp', 'ctx')), may hold values from -4 to 4
- w_in: bfloat16 [8, 768, 3072], P('ctx', 'dp'), may hold values from -0.21875 to 0.21875
- w_out: bfloat16 [8, 3072, 768], P('ctx', 'dp'), may hold values from -3.5 to 3.5
- cotangent: bfloat16 [8, 1024, 768], P('dp', 'ctx'), may hold values from -6 to 6
- segments: int32 [8, 1024], P('dp', 'ctx'), may hold values from -1 to 4, as said below
- buckets: int32 [2047], replicated, may hold values from 0 to 31
- expert_ids: int32 [8, 1024], P('dp', 'ctx'), may hold values from 0 to 7, as said below
- slots: int32 [8, 1024], P('dp', 'ctx'), may hold values from 0 to 28, as said below
Outputs:
- output: bfloat16 [8, 1024, 768], P('dp', 'ctx')
- grad_tokens: float32 [8, 1024, 768], P('dp', 'ctx')
- grad_attn_qkv: float32 [3, 768, 768], P(None, ('dp', 'ctx'))
- grad_attn_out: float32 [768, 768], P(('dp', 'ctx'))
- grad_norm_gains: float32 [2, 768], P(None, ('dp', 'ctx'))
- grad_router: float32 [768, 8], P(('dp', 'ctx'))
- grad_rel_table: float32 [384], P(('dp', 'ctx'))
- grad_w_in: float32 [8, 768, 3072], P('ctx', 'dp')
- grad_w_out: float32 [8, 3072, 768], P('ctx', 'dp')
The draws below stay inside these ranges and needn't reach their ends.
Inputs may be any that keep to these rules, and one draw needn't show every extreme that they name: `segments`: along each sequence the document numbers start at 0 and never fall up to the padding. Of the 2 sequences from each multiple of 2, one is a single document with no padding, each of the others holds five documents, and exactly one of those others ends in 256 padding positions numbered -1. `expert_ids`: A capacity group is the positions of the 1 sequence from a multiple of 1, within one block of 128 positions from a multiple of 128. In a group no two positions share both expert id and slot; padding positions carry ids and slots too. In each capacity group one expert holds slots 0 to 28, the same expert in all groups of the same sequences; the other experts hold slots under 21.
All inputs are finite; a program needn't handle non-finite values.
Results may differ from the reference program's by a relative error of at most 0.02.
Values may be sent and summed in bfloat16 or wider, within the bound.
A program may use at most 192 MiB of HBM per device.

```python
import jax
import jax.numpy as jnp
from jax import lax

D = 768
H = 12
DH = 64
FF = 3072
NB = 32
S_DEV = 128
SEQ_MB = 1
MICRO = 2
EXPERTS = 8
SEQ_DEV = 2
SEQS = 8
LEN = 1024
PAD = 256
CAP = 21
OVER = 8


def route_codes(key):
    groups_dp = SEQS // SEQ_DEV
    parts_ctx = LEN // S_DEV
    group_rows = SEQ_MB * S_DEV
    loaded = CAP + OVER
    first_key = jax.random.fold_in(key, 11)
    first_list = jax.random.randint(first_key, (groups_dp * MICRO,), 0, EXPERTS)
    first_list = jnp.repeat(first_list, parts_ctx)
    group_keys = jax.random.split(jax.random.fold_in(key, 12), groups_dp * MICRO * parts_ctx)

    def one_group(group_key, first_expert):
        rest_key, order_key = jax.random.split(group_key)
        rest_slots = jax.random.permutation(rest_key, (EXPERTS - 1) * CAP)[:group_rows - loaded]
        rest_expert = rest_slots // CAP
        rest_expert = rest_expert + (rest_expert >= first_expert).astype(jnp.int32)
        rest_codes = rest_expert * loaded + rest_slots % CAP
        full_codes = first_expert * loaded + jnp.arange(loaded, dtype=jnp.int32)
        route_list = jnp.concatenate([full_codes, rest_codes])
        return route_list[jax.random.permutation(order_key, group_rows)]
    route_list = jax.vmap(one_group)(group_keys, first_list)
    route_list = route_list.reshape(groups_dp, MICRO, parts_ctx, SEQ_MB, S_DEV)
    route_list = jnp.transpose(route_list, (0, 1, 3, 2, 4)).reshape(SEQS, LEN)
    return (route_list, loaded)


def draw_expert_ids(key, part):
    route_list, loaded = route_codes(key)
    return route_list // loaded


def draw_slots(key, part):
    route_list, loaded = route_codes(key)
    return route_list % loaded


def draw_segments(key, part):
    key = jax.random.fold_in(key, 5)
    pick_key, cut_key, pad_key = jax.random.split(key, 3)
    groups_dp = SEQS // SEQ_DEV
    whole_seq = jax.random.randint(pick_key, (groups_dp,), 0, SEQ_DEV)
    pad_seq = (whole_seq + 1 + jax.random.randint(pad_key, (groups_dp,), 0, SEQ_DEV - 1)) % SEQ_DEV
    seq_range = jnp.tile(jnp.arange(SEQ_DEV, dtype=jnp.int32), groups_dp)
    whole_row = jnp.repeat(whole_seq, SEQ_DEV) == seq_range
    pad_row = jnp.repeat(pad_seq, SEQ_DEV) == seq_range
    row_keys = jax.random.split(cut_key, SEQS)

    def one_row(row_key):
        cut_pos = jax.random.permutation(row_key, LEN - PAD - 1)[:4] + 1
        return jnp.zeros((LEN,), jnp.int32).at[cut_pos].set(1)
    cut_marks = jax.vmap(one_row)(row_keys)
    cut_marks = jnp.where(whole_row[:, None], jnp.zeros_like(cut_marks), cut_marks)
    numbers = jnp.cumsum(cut_marks, axis=1).astype(jnp.int32)
    tail = jnp.arange(LEN, dtype=jnp.int32)[None, :] >= LEN - PAD
    return jnp.where(pad_row[:, None] & tail, -1, numbers).astype(jnp.int32)


def touch_ends(drawn, stream_key, smallest, high):
    shape = drawn.shape
    index_at = [jax.random.randint(jax.random.fold_in(stream_key, axis), (), 0, shape[axis]) for axis in range(len(shape))]
    drawn = drawn.at[tuple(index_at)].set(smallest)
    longest = shape.index(max(shape))
    index_at[longest] = (index_at[longest] + 1) % shape[longest]
    return drawn.at[tuple(index_at)].set(high)


def levels(rng, extent, shards, smallest, high):
    gain, own = 1.0, jax.random.fold_in(rng, 6)
    for dim, parts in shards:
        steps = jnp.exp(jax.random.uniform(jax.random.fold_in(own, dim), (parts,), jnp.float32, smallest / len(shards), high / len(shards)))
        gain = gain * jnp.repeat(steps, extent[dim] // parts).reshape([-1 if axis == dim else 1 for axis in range(len(extent))])
    return gain


def centred(stream_key, extent, scale, most, shards=(), kind=jnp.bfloat16):
    entries = scale * jax.random.normal(stream_key, extent, jnp.float32)
    if shards:
        entries = entries * levels(stream_key, extent, shards, -0.22, 0.18)
    return jnp.clip(entries, -most, most).astype(kind)


def setup_inputs(seed: int = 0) -> dict:
    seeds = jax.random.split(jax.random.key(seed), 14)
    return {
        "tokens": centred(seeds[0], (SEQS, LEN, D), 1.0, 6.0, ((0, 4), (1, 8))),
        "attn_qkv": centred(seeds[1], (3, D, D), D ** -0.5, 0.21875, ((1, 32),)),
        "attn_out": centred(seeds[2], (D, D), (D // 64) ** -0.5, 1.75, ((0, 32),)),
        "norm_gains": jnp.clip(1.0 + 0.1 * jax.random.normal(seeds[3], (2, D), jnp.float32), 0.5, 1.5).astype(jnp.bfloat16),
        "router": centred(seeds[4], (D, EXPERTS), (4 * D) ** -0.5, 0.109375, ((0, 32),)),
        "rel_table": centred(seeds[5], (NB * H,), 1.0, 4.0, ((0, 32),)),
        "w_in": centred(seeds[6], (EXPERTS, D, FF), D ** -0.5, 0.21875, ((0, 8), (1, 4))),
        "w_out": centred(seeds[7], (EXPERTS, FF, D), (max(FF // 1024, 1)) ** -0.5, 3.5, ((0, 8), (1, 4))),
        "cotangent": centred(seeds[8], (SEQS, LEN, D), 1.0, 6.0, ((0, 4), (1, 8))),
        "segments": draw_segments(jax.random.fold_in(seeds[13], 71), 0),
        "buckets": touch_ends(jax.random.randint(seeds[10], (2 * LEN - 1,), 0, NB), jax.random.fold_in(seeds[10], 1), 0, NB - 1).astype(jnp.int32),
        "expert_ids": draw_expert_ids(jax.random.fold_in(seeds[13], 71), 0),
        "slots": draw_slots(jax.random.fold_in(seeds[13], 71), 0),
    }


epsilon = 1e-06
precise = lax.Precision.HIGHEST
masked_score = -1000000000.0

@jax.custom_vjp
def low(v):
    return lax.optimization_barrier(v.astype(jnp.bfloat16)).astype(jnp.float32)

@jax.custom_vjp
def low_back(v):
    return v

def low_keep(v):
    return (low(v), None)

def low_pass(kept, grad):
    return (grad,)

def back_keep(v):
    return (v, None)

def back_low(kept, grad):
    return (low(grad),)
low.defvjp(low_keep, low_pass)
low_back.defvjp(back_keep, back_low)

def both_ways(value_in):
    return low(low_back(value_in))

def rms_scale(values, gain_row):
    return values * lax.rsqrt(lax.optimization_barrier(jnp.mean(values * values, axis=-1, keepdims=True)) + epsilon) * gain_row

def to_groups(array):
    tail = array.shape[2:]
    grouped = array.reshape((SEQS // SEQ_MB, SEQ_MB, LEN // S_DEV, S_DEV) + tail)
    grouped = jnp.swapaxes(grouped, 1, 2)
    return grouped.reshape((SEQS * LEN // (SEQ_MB * S_DEV), SEQ_MB * S_DEV) + tail)

def from_groups(array):
    tail = array.shape[2:]
    grouped = array.reshape((SEQS // SEQ_MB, LEN // S_DEV, SEQ_MB, S_DEV) + tail)
    grouped = jnp.swapaxes(grouped, 1, 2)
    return grouped.reshape((SEQS, LEN) + tail)

def reference(tokens, attn_qkv, attn_out, norm_gains, router, rel_table, w_in, w_out, cotangent, segments, buckets, expert_ids, slots):
    score_scale = DH ** (-0.5)
    slot_total = EXPERTS * CAP
    group_count = SEQS * LEN // (SEQ_MB * S_DEV)
    positions = jnp.arange(LEN, dtype=jnp.int32)
    bucket_grid = buckets[positions[:, None] - positions[None, :] + LEN - 1]
    live_rows = segments >= 0
    group_codes = to_groups(expert_ids * CAP + slots)
    group_kept = to_groups((slots < CAP) & live_rows)
    targets = jnp.where(group_kept, group_codes, slot_total)
    safe_codes = jnp.minimum(targets, slot_total - 1)
    pick_mask = (expert_ids[..., None] == jnp.arange(EXPERTS, dtype=jnp.int32)).astype(jnp.float32)

    def attend(seq_normed, seq_segments, qkv_weight, score_bias):
        projected = both_ways(jnp.einsum('td,pde->pte', seq_normed, qkv_weight, precision=precise))
        queries = projected[0].reshape(LEN, H, DH)
        keys_all = projected[1].reshape(LEN, H, DH)
        values_all = projected[2].reshape(LEN, H, DH)
        raw = jnp.einsum('qhd,khd->hqk', queries, keys_all, precision=precise) * score_scale + score_bias
        raw = low_back(raw)
        same = seq_segments[:, None] == seq_segments[None, :]
        raw = jnp.where(same[None], raw, masked_score)
        prob_rows = jax.nn.softmax(raw, axis=-1)
        mixed = jnp.einsum('hqk,khd->qhd', low(prob_rows), values_all, precision=precise)
        return both_ways(mixed.reshape(LEN, D))
    attend_saved = jax.checkpoint(attend)

    def expert_run(rows_in, weight_in, weight_out):
        expert_pre = low_back(jnp.dot(rows_in, weight_in, precision=precise))
        expert_act = low(jax.nn.gelu(expert_pre, approximate=True))
        return both_ways(jnp.dot(expert_act, weight_out, precision=precise))
    expert_saved = jax.checkpoint(expert_run)

    def fill_group(rows_x, rows_target):
        return jnp.zeros((slot_total, D), rows_x.dtype).at[rows_target].set(rows_x, mode='drop')

    def forward(tokens_f, qkv_f, out_f, gains_f, router_f, table_f, win_f, wout_f):
        table_grid = table_f.reshape(NB, H)
        score_bias = jnp.transpose(table_grid[bucket_grid], (2, 0, 1))
        normed = low(rms_scale(tokens_f, gains_f[0]))

        def per_sequence(inputs):
            return attend_saved(inputs[0], inputs[1], qkv_f, score_bias)
        attended = lax.map(per_sequence, (normed, segments))
        branch = low_back(jnp.einsum('std,de->ste', attended, out_f, precision=precise))
        hidden = tokens_f + branch
        normed2 = low(rms_scale(hidden, gains_f[1]))
        gate_probs = jax.nn.softmax(jnp.einsum('std,de->ste', normed2, router_f, precision=precise), axis=-1)
        chosen = lax.optimization_barrier(jnp.sum(gate_probs * pick_mask, axis=-1))
        expert_in = to_groups(low_back(normed2))
        buffers = jax.vmap(fill_group)(expert_in, targets)
        per_expert = jnp.swapaxes(buffers.reshape(group_count, EXPERTS, CAP, D), 0, 1).reshape(EXPERTS, group_count * CAP, D)

        def per_weight(inputs):
            return expert_saved(inputs[0], inputs[1], inputs[2])
        produced = lax.map(per_weight, (per_expert, win_f, wout_f))
        returned = jnp.swapaxes(produced.reshape(EXPERTS, group_count, CAP, D), 0, 1).reshape(group_count, slot_total, D)
        picked = jnp.take_along_axis(returned, safe_codes[..., None], axis=1)
        picked = jnp.where(group_kept[..., None], picked, jnp.zeros_like(picked))
        return hidden + chosen[..., None] * from_groups(picked)
    result, pullback = jax.vjp(forward, tokens.astype(jnp.float32), attn_qkv.astype(jnp.float32), attn_out.astype(jnp.float32), norm_gains.astype(jnp.float32), router.astype(jnp.float32), rel_table.astype(jnp.float32), w_in.astype(jnp.float32), w_out.astype(jnp.float32))
    grad_output = cotangent.astype(jnp.float32) * live_rows[..., None].astype(jnp.float32)
    grads = pullback(grad_output)
    return (result.astype(jnp.bfloat16), grads[0], grads[1], grads[2], grads[3], grads[4], grads[5], grads[6], grads[7])
```

```python
import jax
import jax.numpy as jnp
from jax import lax
from jax.experimental import pallas as pl
from jax.experimental.pallas import tpu as pltpu
from jax.sharding import PartitionSpec as P

H = 12
DH = 64
FF = 3072
NB = 32

epsilon = 1e-06
precise = lax.Precision.HIGHEST
masked_score = -1000000000.0
bf16 = jnp.bfloat16
f32 = jnp.float32
VMEM_LIMIT = 50 * 1024 * 1024


def rms_scale(values, gain_row):
    return (
        values * lax.rsqrt(jnp.mean(values * values, axis=-1, keepdims=True) + epsilon) * gain_row
    )


def gelu_tanh(values):
    return jax.nn.gelu(values, approximate=True)


def dot(a, b, ca, cb):
    return lax.dot_general(a, b, (((ca,), (cb,)), ((), ())), preferred_element_type=f32)


def attend_kernel(qkv_ref, base_ref, segq_ref, segk_ref, p_ref, mixed_ref, bias_ref):
    length = qkv_ref.shape[3]
    block = bias_ref.shape[0]
    bias_ref[0:8, :] = base_ref[0]
    rows = 8
    while rows < block:
        bias_ref[rows : 2 * rows, :] = pltpu.roll(bias_ref[0:rows, :], rows, 1)
        rows *= 2
    keys = qkv_ref[1, 0]
    vals = qkv_ref[2, 0]
    seg_keys = segk_ref[...]

    def step(b, carry):
        at = pl.ds(pl.multiple_of(b * block, block), block)
        shift = pl.ds(pl.multiple_of(length - block - b * block, block), length)
        scores = dot(qkv_ref[0, 0, :, at], keys, 0, 0) + bias_ref[:, shift]
        scores = jnp.where(segq_ref[at, :] == seg_keys, scores, masked_score)
        peak = jnp.max(scores, axis=-1, keepdims=True)
        shifted = jnp.exp(scores - peak)
        total = jnp.sum(shifted, axis=-1, keepdims=True)
        probs = (shifted * (1.0 / total)).astype(bf16)
        p_ref[0, at, :] = probs
        mixed_ref[b, 0] = dot(vals, probs, 1, 1).astype(bf16)
        return carry

    lax.fori_loop(0, length // block, step, 0)


def attend(qkv, base, seg, block):
    heads, length = qkv.shape[1], qkv.shape[3]
    count = length // block
    return pl.pallas_call(
        attend_kernel,
        grid=(heads,),
        in_specs=[
            pl.BlockSpec((3, 1, DH, length), lambda h: (0, h, 0, 0)),
            pl.BlockSpec((1, 8, 2 * length), lambda h: (h, 0, 0)),
            pl.BlockSpec((length, 1), lambda h: (0, 0)),
            pl.BlockSpec((1, length), lambda h: (0, 0)),
        ],
        out_specs=[
            pl.BlockSpec((1, length, length), lambda h: (h, 0, 0)),
            pl.BlockSpec((count, 1, DH, block), lambda h: (0, h, 0, 0)),
        ],
        out_shape=[
            jax.ShapeDtypeStruct((heads, length, length), bf16),
            jax.ShapeDtypeStruct((count, heads, DH, block), bf16),
        ],
        scratch_shapes=[pltpu.VMEM((block, 2 * length), f32)],
        compiler_params=pltpu.CompilerParams(vmem_limit_bytes=VMEM_LIMIT),
        cost_estimate=pl.CostEstimate(
            flops=4 * heads * length * length * DH,
            bytes_accessed=2 * heads * length * length,
            transcendentals=heads * length * length,
        ),
    )(qkv, base, seg[:, None], seg[None, :])


def attend_back_kernel(qkv_ref, p_ref, gm_ref, g_ref, diag_ref, acc_ref, gk_ref, gv_ref):
    length = qkv_ref.shape[3]
    block = acc_ref.shape[0]
    acc_ref[...] = jnp.zeros_like(acc_ref)
    gk_ref[...] = jnp.zeros_like(gk_ref)
    gv_ref[...] = jnp.zeros_like(gv_ref)
    keys = qkv_ref[1, 0]
    vals = qkv_ref[2, 0]

    def step(b, carry):
        at = pl.ds(pl.multiple_of(b * block, block), block)
        shift = pl.ds(pl.multiple_of(length - block - b * block, block), length)
        gm = gm_ref[b, 0]
        probs_low = p_ref[0, at, :]
        probs = probs_low.astype(f32)
        weighed = probs * dot(gm, vals, 0, 0)
        delta = jnp.sum(weighed, axis=-1, keepdims=True)
        gs = weighed - probs * delta
        gs_low = gs.astype(bf16)
        acc_ref[:, shift] += gs
        g_ref[0, 0, :, at] = (dot(keys, gs_low, 1, 1) * (DH**-0.5)).astype(bf16)
        gk_ref[...] += dot(qkv_ref[0, 0, :, at], gs_low, 1, 0)
        gv_ref[...] += dot(gm, probs_low, 1, 0)
        return carry

    lax.fori_loop(0, length // block, step, 0)
    g_ref[1, 0] = gk_ref[...].astype(bf16)
    g_ref[2, 0] = gv_ref[...].astype(bf16)
    rows = block // 2
    while rows >= 8:
        acc_ref[0:rows, :] += pltpu.roll(acc_ref[rows : 2 * rows, :], 2 * length - rows, 1)
        rows //= 2
    diag_ref[0] = acc_ref[0:8, :]


def attend_back(qkv, probs, gm):
    heads, length = qkv.shape[1], qkv.shape[3]
    count, block = gm.shape[0], gm.shape[3]
    return pl.pallas_call(
        attend_back_kernel,
        grid=(heads,),
        in_specs=[
            pl.BlockSpec((3, 1, DH, length), lambda h: (0, h, 0, 0)),
            pl.BlockSpec((1, length, length), lambda h: (h, 0, 0)),
            pl.BlockSpec((count, 1, DH, block), lambda h: (0, h, 0, 0)),
        ],
        out_specs=[
            pl.BlockSpec((3, 1, DH, length), lambda h: (0, h, 0, 0)),
            pl.BlockSpec((1, 8, 2 * length), lambda h: (h, 0, 0)),
        ],
        out_shape=[
            jax.ShapeDtypeStruct((3, heads, DH, length), bf16),
            jax.ShapeDtypeStruct((heads, 8, 2 * length), f32),
        ],
        scratch_shapes=[
            pltpu.VMEM((block, 2 * length), f32),
            pltpu.VMEM((DH, length), f32),
            pltpu.VMEM((DH, length), f32),
        ],
        compiler_params=pltpu.CompilerParams(vmem_limit_bytes=VMEM_LIMIT),
        cost_estimate=pl.CostEstimate(
            flops=8 * heads * length * length * DH,
            bytes_accessed=2 * heads * length * length,
            transcendentals=0,
        ),
    )(qkv, probs, gm)


def pad_last(values, size):
    widths = [(0, 0)] * (values.ndim - 1) + [(0, size - values.shape[-1])]
    return jnp.pad(values, widths)


def swap(values, axis):
    return lax.all_to_all(values, axis, split_axis=0, concat_axis=0, tiled=True)


def on_device(
    tokens,
    attn_qkv,
    attn_out,
    norm_gains,
    router,
    rel_table,
    w_in,
    w_out,
    cotangent,
    segments,
    buckets,
    expert_ids,
    slots,
):
    ctx_count = lax.axis_size("ctx")
    dp_count = lax.axis_size("dp")
    ctx_index = lax.axis_index("ctx")
    seqs, block, width = tokens.shape
    length = ctx_count * block
    experts = ctx_count * w_in.shape[0]
    own_rows = attn_qkv.shape[1]
    table_rows = rel_table.shape[0]
    groups = ctx_count // seqs
    heads = -(-H // groups)
    cols = heads * DH
    all_cols = groups * cols
    my_seq = ctx_index // groups
    my_group = ctx_index % groups
    capacity = block * 4 // (3 * experts)
    cap_pad = -(-capacity // 8) * 8
    slot_total = experts * cap_pad
    ff_part = FF // dp_count

    qkv_cols = (
        pad_last(attn_qkv, all_cols)
        .reshape(3, own_rows, groups, cols)
        .transpose(2, 1, 0, 3)
        .reshape(groups, own_rows, 3 * cols)
    )
    table_col = jnp.pad(rel_table, (0, own_rows - table_rows))[:, None]
    small = pad_last(jnp.concatenate([norm_gains.T, router, table_col], axis=1), 128)
    packed = jnp.concatenate(
        [qkv_cols, jnp.broadcast_to(small[None], (groups,) + small.shape)], axis=2
    )
    packed = swap(jnp.concatenate([packed] * seqs, axis=0), "ctx")
    layer = lax.all_gather(packed, "dp", axis=0, tiled=False).reshape(width, -1)
    w_heads = layer[:, : 3 * cols]
    rest = layer[:, 3 * cols :]
    gain_first = rest[:, 0].astype(f32)
    gain_second = rest[:, 1].astype(f32)
    router_full = rest[:, 2 : 2 + experts]
    table = rest[:, 2 + experts].reshape(-1, own_rows)[:, :table_rows].reshape(NB, H)

    seg_rows = jnp.pad(
        segments.astype(bf16)[:, None, :], ((0, 0), (0, 15), (0, width - block))
    )
    spread = lax.all_gather(
        jnp.concatenate([tokens, seg_rows], axis=1), "ctx", axis=0, tiled=False
    )
    spread = lax.dynamic_index_in_dim(spread, my_seq, axis=1, keepdims=False)
    x_seq = spread[:, :block].reshape(length, width).astype(f32)
    seg_seq = spread[:, block, :block].reshape(length).astype(jnp.int32)

    out_full = lax.all_gather(attn_out, ("dp", "ctx"), axis=0, tiled=True)
    win_part = swap(
        w_in[0].reshape(-1, dp_count, ff_part).transpose(1, 0, 2), "dp"
    ).reshape(width, ff_part)
    wout_part = w_out[0]

    bucket_line = jnp.pad(jnp.flip(buckets), (0, 1), constant_values=-1)
    onehot_line = (bucket_line[:, None] == jnp.arange(NB, dtype=jnp.int32)).astype(bf16)
    table_part = lax.dynamic_slice_in_dim(
        pad_last(table, groups * heads), my_group * heads, heads, axis=1
    )
    bias_line = jnp.einsum("wn,nh->hw", onehot_line, table_part, preferred_element_type=f32)
    bias_base = jnp.stack(
        [jnp.roll(bias_line, a + 1 - block, axis=1) for a in range(8)], axis=1
    )

    normed_seq = rms_scale(x_seq, gain_first).astype(bf16)
    projected = dot(w_heads, normed_seq, 0, 1).astype(bf16).reshape(3, heads, DH, length)
    scale = jnp.array([DH**-0.5, 1.0, 1.0], bf16)[:, None, None, None]
    projected = projected * scale
    probs, mixed_parts = attend(projected, bias_base, seg_seq, block)
    mixed = swap(mixed_parts.reshape(ctx_count, cols, block), "ctx")
    mixed = mixed.reshape(seqs, all_cols, block)[:, :width]

    live = segments >= 0
    x_float = tokens.astype(f32)
    branch = jnp.einsum("bds,de->bse", mixed, out_full, preferred_element_type=f32)
    hidden = x_float + branch
    normed2 = rms_scale(hidden, gain_second).astype(bf16)
    logits = jnp.einsum("bsd,de->bse", normed2, router_full, preferred_element_type=f32)
    gate_probs = jax.nn.softmax(logits, axis=-1)
    expert_range = jnp.arange(experts, dtype=jnp.int32)
    pick_mask = (expert_ids[..., None] == expert_range).astype(f32)
    chosen = jnp.sum(gate_probs * pick_mask, axis=-1)
    grad_out = cotangent.astype(f32) * live[..., None].astype(f32)
    grad_picked = (chosen[..., None] * grad_out).astype(bf16)
    kept = (slots < capacity) & live
    target = jnp.where(kept, expert_ids * cap_pad + slots, slot_total)
    place = (
        target[:, None, :] == jnp.arange(slot_total, dtype=jnp.int32)[None, :, None]
    ).astype(bf16)

    def to_slots(rows):
        moved = jnp.einsum("bcr,brd->bcd", place, rows, preferred_element_type=f32)
        moved = moved.astype(bf16).reshape(seqs, experts, cap_pad, width)
        return moved.transpose(1, 0, 2, 3).reshape(experts, seqs * cap_pad, width)

    def from_slots(rows):
        rows = rows.reshape(experts, seqs, cap_pad, width).transpose(1, 0, 2, 3)
        rows = rows.reshape(seqs, slot_total, width)
        return jnp.einsum("bcr,bcd->brd", place, rows, preferred_element_type=f32)

    slot_rows = seqs * cap_pad
    arrived = swap(jnp.concatenate([to_slots(normed2), to_slots(grad_picked)], axis=1), "ctx")
    rows_in = lax.all_gather(arrived[:, :slot_rows], "dp", axis=0, tiled=False)
    grads_in = lax.all_gather(arrived[:, slot_rows:], "dp", axis=0, tiled=False)
    rows_in = rows_in.reshape(-1, width)
    grads_in = grads_in.reshape(-1, width)

    expert_pre = dot(rows_in, win_part, 1, 0)
    expert_act = gelu_tanh(expert_pre).astype(bf16)
    produced = lax.psum_scatter(
        dot(expert_act, wout_part, 1, 0).astype(bf16), "dp", scatter_dimension=0, tiled=True
    )
    grad_act = dot(grads_in, wout_part, 1, 1)
    grad_pre = jax.vjp(gelu_tanh, expert_pre)[1](grad_act)[0].astype(bf16)
    grad_sent = lax.psum_scatter(
        dot(grad_pre, win_part, 1, 1).astype(bf16), "dp", scatter_dimension=0, tiled=True
    )
    grad_wout = dot(expert_act, grads_in, 0, 0)
    grad_win = dot(rows_in, grad_pre, 0, 0).astype(bf16)
    grad_win = swap(grad_win.reshape(dp_count, -1, ff_part), "dp").astype(f32)
    grad_win = grad_win.transpose(1, 0, 2).reshape(-1, FF)

    returned = swap(
        jnp.concatenate(
            [
                produced.reshape(ctx_count, slot_rows, width),
                grad_sent.reshape(ctx_count, slot_rows, width),
            ],
            axis=1,
        ),
        "ctx",
    )
    picked = from_slots(returned[:, :slot_rows])
    grad_expert_in = from_slots(returned[:, slot_rows:])
    output = (hidden + chosen[..., None] * picked).astype(bf16)

    grad_chosen = jnp.sum(grad_out * picked, axis=-1)
    grad_logits = gate_probs * (
        grad_chosen[..., None] * pick_mask - (grad_chosen * chosen)[..., None]
    )
    sum_router = jnp.einsum("bsd,bse->de", normed2.astype(f32), grad_logits, precision=precise)
    grad_normed2 = grad_expert_in + jnp.einsum(
        "bse,de->bsd", grad_logits, router_full.astype(f32), precision=precise
    )
    grad_hidden_norm, sum_gain_second = jax.vjp(rms_scale, hidden, gain_second)[1](grad_normed2)
    grad_hidden = grad_out + grad_hidden_norm
    grad_branch = grad_hidden.astype(bf16)
    grad_mixed = jnp.einsum(
        "bse,de->bds", grad_branch, out_full, preferred_element_type=f32
    ).astype(bf16)
    grad_mixed = jnp.pad(grad_mixed, ((0, 0), (0, all_cols - width), (0, 0)))
    grad_mixed = swap(grad_mixed.reshape(ctx_count, cols, block), "ctx")
    sum_out = jnp.einsum("bds,bse->de", mixed, grad_branch, preferred_element_type=f32)
    grad_attn_out = lax.psum_scatter(
        sum_out.astype(bf16), ("dp", "ctx"), scatter_dimension=0, tiled=True
    ).astype(f32)

    grad_parts, diag = attend_back(
        projected, probs, grad_mixed.reshape(ctx_count, heads, DH, block)
    )
    grad_parts = grad_parts.reshape(3 * cols, length)
    normed_part = dot(grad_parts, w_heads, 0, 1).astype(bf16)
    normed_part = swap(normed_part.reshape(ctx_count, block, width), "ctx")
    grad_normed = jnp.sum(
        normed_part.reshape(seqs, groups, block, width).astype(f32), axis=1
    )
    sum_qkv = lax.psum_scatter(
        dot(normed_seq, grad_parts, 0, 1).astype(bf16), "dp", scatter_dimension=0, tiled=True
    )
    sum_qkv = swap(sum_qkv.reshape(ctx_count, own_rows, 3 * cols), "ctx").astype(f32)
    sum_qkv = jnp.sum(sum_qkv.reshape(seqs, groups, own_rows, 3, cols), axis=0)
    grad_attn_qkv = sum_qkv.transpose(2, 1, 0, 3).reshape(3, own_rows, all_cols)[..., :width]

    grad_x_norm, sum_gain_first = jax.vjp(rms_scale, x_float, gain_first)[1](grad_normed)
    grad_tokens = grad_hidden + grad_x_norm

    diag_line = sum(
        jnp.roll(diag[:, a, :], block - 1 - a, axis=1) for a in range(8)
    )
    sum_table = jnp.einsum(
        "wn,hw->nh", onehot_line.astype(f32), diag_line, precision=precise
    )
    sum_table = lax.dynamic_update_slice_in_dim(
        jnp.zeros((NB, groups * heads), f32), sum_table, my_group * heads, axis=1
    )[:, :H]
    table_col = pad_last(sum_table.reshape(-1, table_rows), own_rows).reshape(width, 1)
    sums = lax.psum_scatter(
        jnp.concatenate(
            [sum_gain_first[:, None], sum_gain_second[:, None], sum_router, table_col], axis=1
        ),
        ("dp", "ctx"),
        scatter_dimension=0,
        tiled=True,
    )
    return (
        output,
        grad_tokens,
        grad_attn_qkv,
        grad_attn_out,
        sums[:, :2].T,
        sums[:, 2 : 2 + experts],
        sums[:table_rows, 2 + experts],
        grad_win[None],
        grad_wout[None],
    )


def solution(mesh):
    in_specs = (
        P("dp", "ctx", None),
        P(None, ("dp", "ctx"), None),
        P(("dp", "ctx"), None),
        P(None, ("dp", "ctx")),
        P(("dp", "ctx"), None),
        P(("dp", "ctx")),
        P("ctx", "dp", None),
        P("ctx", "dp", None),
        P("dp", "ctx", None),
        P("dp", "ctx"),
        P(),
        P("dp", "ctx"),
        P("dp", "ctx"),
    )
    out_specs = (
        P("dp", "ctx", None),
        P("dp", "ctx", None),
        P(None, ("dp", "ctx"), None),
        P(("dp", "ctx"), None),
        P(None, ("dp", "ctx")),
        P(("dp", "ctx"), None),
        P(("dp", "ctx")),
        P("ctx", "dp", None),
        P("ctx", "dp", None),
    )
    return jax.shard_map(
        on_device, mesh=mesh, in_specs=in_specs, out_specs=out_specs, check_vma=False
    )
```

```python
import jax
import jax.numpy as jnp
from jax import lax
from jax.experimental import pallas as pl
from jax.experimental.pallas import tpu as pltpu
from jax.sharding import PartitionSpec as P

H = 12
DH = 64
FF = 3072
NB = 32

epsilon = 1e-06
precise = lax.Precision.HIGHEST
masked_score = -1000000000.0
bf16 = jnp.bfloat16
f32 = jnp.float32
VMEM_LIMIT = 50 * 1024 * 1024


def rms_scale(values, gain_row):
    return (
        values * lax.rsqrt(jnp.mean(values * values, axis=-1, keepdims=True) + epsilon) * gain_row
    )


def gelu_tanh(values):
    return jax.nn.gelu(values, approximate=True)


def dot(a, b, ca, cb):
    return lax.dot_general(a, b, (((ca,), (cb,)), ((), ())), preferred_element_type=f32)


def attend_kernel(qkv_ref, base_ref, segq_ref, segk_ref, p_ref, mixed_ref, bias_ref):
    length = qkv_ref.shape[3]
    block = bias_ref.shape[0]
    bias_ref[0:8, :] = base_ref[0]
    rows = 8
    while rows < block:
        bias_ref[rows : 2 * rows, :] = pltpu.roll(bias_ref[0:rows, :], rows, 1)
        rows *= 2
    keys = qkv_ref[1, 0]
    vals = qkv_ref[2, 0]
    seg_keys = segk_ref[...]

    def step(b, carry):
        at = pl.ds(pl.multiple_of(b * block, block), block)
        shift = pl.ds(pl.multiple_of(length - block - b * block, block), length)
        scores = dot(qkv_ref[0, 0, :, at], keys, 0, 0) + bias_ref[:, shift]
        scores = jnp.where(segq_ref[at, :] == seg_keys, scores, masked_score)
        peak = jnp.max(scores, axis=-1, keepdims=True)
        shifted = jnp.exp(scores - peak)
        total = jnp.sum(shifted, axis=-1, keepdims=True)
        probs = (shifted * (1.0 / total)).astype(bf16)
        p_ref[0, at, :] = probs
        mixed_ref[b, 0] = dot(vals, probs, 1, 1).astype(bf16)
        return carry

    lax.fori_loop(0, length // block, step, 0)


def attend(qkv, base, seg, block):
    heads, length = qkv.shape[1], qkv.shape[3]
    count = length // block
    return pl.pallas_call(
        attend_kernel,
        grid=(heads,),
        in_specs=[
            pl.BlockSpec((3, 1, DH, length), lambda h: (0, h, 0, 0)),
            pl.BlockSpec((1, 8, 2 * length), lambda h: (h, 0, 0)),
            pl.BlockSpec((length, 1), lambda h: (0, 0)),
            pl.BlockSpec((1, length), lambda h: (0, 0)),
        ],
        out_specs=[
            pl.BlockSpec((1, length, length), lambda h: (h, 0, 0)),
            pl.BlockSpec((count, 1, DH, block), lambda h: (0, h, 0, 0)),
        ],
        out_shape=[
            jax.ShapeDtypeStruct((heads, length, length), bf16),
            jax.ShapeDtypeStruct((count, heads, DH, block), bf16),
        ],
        scratch_shapes=[pltpu.VMEM((block, 2 * length), f32)],
        compiler_params=pltpu.CompilerParams(vmem_limit_bytes=VMEM_LIMIT),
        cost_estimate=pl.CostEstimate(
            flops=4 * heads * length * length * DH,
            bytes_accessed=2 * heads * length * length,
            transcendentals=heads * length * length,
        ),
    )(qkv, base, seg[:, None], seg[None, :])


def attend_back_kernel(qkv_ref, p_ref, gm_ref, g_ref, diag_ref, acc_ref, gk_ref, gv_ref):
    length = qkv_ref.shape[3]
    block = acc_ref.shape[0]
    acc_ref[...] = jnp.zeros_like(acc_ref)
    gk_ref[...] = jnp.zeros_like(gk_ref)
    gv_ref[...] = jnp.zeros_like(gv_ref)
    keys = qkv_ref[1, 0]
    vals = qkv_ref[2, 0]

    def step(b, carry):
        at = pl.ds(pl.multiple_of(b * block, block), block)
        shift = pl.ds(pl.multiple_of(length - block - b * block, block), length)
        gm = gm_ref[b, 0]
        probs_low = p_ref[0, at, :]
        probs = probs_low.astype(f32)
        weighed = probs * dot(gm, vals, 0, 0)
        delta = jnp.sum(weighed, axis=-1, keepdims=True)
        gs = weighed - probs * delta
        gs_low = gs.astype(bf16)
        acc_ref[:, shift] += gs
        g_ref[0, 0, :, at] = (dot(keys, gs_low, 1, 1) * (DH**-0.5)).astype(bf16)
        gk_ref[...] += dot(qkv_ref[0, 0, :, at], gs_low, 1, 0)
        gv_ref[...] += dot(gm, probs_low, 1, 0)
        return carry

    lax.fori_loop(0, length // block, step, 0)
    g_ref[1, 0] = gk_ref[...].astype(bf16)
    g_ref[2, 0] = gv_ref[...].astype(bf16)
    rows = block // 2
    while rows >= 8:
        acc_ref[0:rows, :] += pltpu.roll(acc_ref[rows : 2 * rows, :], 2 * length - rows, 1)
        rows //= 2
    diag_ref[0] = acc_ref[0:8, :]


def attend_back(qkv, probs, gm):
    heads, length = qkv.shape[1], qkv.shape[3]
    count, block = gm.shape[0], gm.shape[3]
    return pl.pallas_call(
        attend_back_kernel,
        grid=(heads,),
        in_specs=[
            pl.BlockSpec((3, 1, DH, length), lambda h: (0, h, 0, 0)),
            pl.BlockSpec((1, length, length), lambda h: (h, 0, 0)),
            pl.BlockSpec((count, 1, DH, block), lambda h: (0, h, 0, 0)),
        ],
        out_specs=[
            pl.BlockSpec((3, 1, DH, length), lambda h: (0, h, 0, 0)),
            pl.BlockSpec((1, 8, 2 * length), lambda h: (h, 0, 0)),
        ],
        out_shape=[
            jax.ShapeDtypeStruct((3, heads, DH, length), bf16),
            jax.ShapeDtypeStruct((heads, 8, 2 * length), f32),
        ],
        scratch_shapes=[
            pltpu.VMEM((block, 2 * length), f32),
            pltpu.VMEM((DH, length), f32),
            pltpu.VMEM((DH, length), f32),
        ],
        compiler_params=pltpu.CompilerParams(vmem_limit_bytes=VMEM_LIMIT),
        cost_estimate=pl.CostEstimate(
            flops=8 * heads * length * length * DH,
            bytes_accessed=2 * heads * length * length,
            transcendentals=0,
        ),
    )(qkv, probs, gm)


def pad_last(values, size):
    widths = [(0, 0)] * (values.ndim - 1) + [(0, size - values.shape[-1])]
    return jnp.pad(values, widths)


def swap(values, axis):
    return lax.all_to_all(values, axis, split_axis=0, concat_axis=0, tiled=True)


def on_device(
    tokens,
    attn_qkv,
    attn_out,
    norm_gains,
    router,
    rel_table,
    w_in,
    w_out,
    cotangent,
    segments,
    buckets,
    expert_ids,
    slots,
):
    ctx_count = lax.axis_size("ctx")
    dp_count = lax.axis_size("dp")
    ctx_index = lax.axis_index("ctx")
    seqs, block, width = tokens.shape
    length = ctx_count * block
    experts = ctx_count * w_in.shape[0]
    own_rows = attn_qkv.shape[1]
    table_rows = rel_table.shape[0]
    groups = ctx_count // seqs
    heads = -(-H // groups)
    cols = heads * DH
    all_cols = groups * cols
    my_seq = ctx_index // groups
    my_group = ctx_index % groups
    capacity = block * 4 // (3 * experts)
    cap_pad = -(-capacity // 8) * 8
    slot_total = experts * cap_pad
    ff_part = FF // dp_count

    qkv_cols = (
        pad_last(attn_qkv, all_cols)
        .reshape(3, own_rows, groups, cols)
        .transpose(2, 1, 0, 3)
        .reshape(groups, own_rows, 3 * cols)
    )
    table_col = jnp.pad(rel_table, (0, own_rows - table_rows))[:, None]
    small = pad_last(jnp.concatenate([norm_gains.T, router, table_col], axis=1), 128)
    packed = jnp.concatenate(
        [qkv_cols, jnp.broadcast_to(small[None], (groups,) + small.shape)], axis=2
    )
    packed = swap(jnp.concatenate([packed] * seqs, axis=0), "ctx")
    layer = lax.all_gather(packed, "dp", axis=0, tiled=False).reshape(width, -1)
    w_heads = layer[:, : 3 * cols]
    rest = layer[:, 3 * cols :]
    gain_first = rest[:, 0].astype(f32)
    gain_second = rest[:, 1].astype(f32)
    router_full = rest[:, 2 : 2 + experts]
    table = rest[:, 2 + experts].reshape(-1, own_rows)[:, :table_rows].reshape(NB, H)

    seg_rows = jnp.pad(
        segments.astype(bf16)[:, None, :], ((0, 0), (0, 15), (0, width - block))
    )
    spread = lax.all_gather(
        jnp.concatenate([tokens, seg_rows], axis=1), "ctx", axis=0, tiled=False
    )
    spread = lax.dynamic_index_in_dim(spread, my_seq, axis=1, keepdims=False)
    x_seq = spread[:, :block].reshape(length, width).astype(f32)
    seg_seq = spread[:, block, :block].reshape(length).astype(jnp.int32)

    out_full = lax.all_gather(attn_out, "dp", axis=0, tiled=False)
    out_full = lax.all_gather(out_full, "ctx", axis=1, tiled=False).reshape(width, width)
    win_part = swap(
        w_in[0].reshape(-1, dp_count, ff_part).transpose(1, 0, 2), "dp"
    ).reshape(width, ff_part)
    wout_part = w_out[0]

    bucket_line = jnp.pad(jnp.flip(buckets), (0, 1), constant_values=-1)
    onehot_line = (bucket_line[:, None] == jnp.arange(NB, dtype=jnp.int32)).astype(bf16)
    table_part = lax.dynamic_slice_in_dim(
        pad_last(table, groups * heads), my_group * heads, heads, axis=1
    )
    bias_line = jnp.einsum("wn,nh->hw", onehot_line, table_part, preferred_element_type=f32)
    bias_base = jnp.stack(
        [jnp.roll(bias_line, a + 1 - block, axis=1) for a in range(8)], axis=1
    )

    normed_seq = rms_scale(x_seq, gain_first).astype(bf16)
    normed_seq, win_part = lax.optimization_barrier((normed_seq, win_part))
    projected = dot(w_heads, normed_seq, 0, 1).astype(bf16).reshape(3, heads, DH, length)
    scale = jnp.array([DH**-0.5, 1.0, 1.0], bf16)[:, None, None, None]
    projected = projected * scale
    probs, mixed_parts = attend(projected, bias_base, seg_seq, block)
    mixed = swap(mixed_parts.reshape(ctx_count, cols, block), "ctx")
    mixed = mixed.reshape(seqs, all_cols, block)[:, :width]

    live = segments >= 0
    x_float = tokens.astype(f32)
    branch = jnp.einsum("bds,de->bse", mixed, out_full, preferred_element_type=f32)
    hidden = x_float + branch
    normed2 = rms_scale(hidden, gain_second).astype(bf16)
    logits = jnp.einsum("bsd,de->bse", normed2, router_full, preferred_element_type=f32)
    gate_probs = jax.nn.softmax(logits, axis=-1)
    expert_range = jnp.arange(experts, dtype=jnp.int32)
    pick_mask = (expert_ids[..., None] == expert_range).astype(f32)
    chosen = jnp.sum(gate_probs * pick_mask, axis=-1)
    grad_out = cotangent.astype(f32) * live[..., None].astype(f32)
    grad_picked = (chosen[..., None] * grad_out).astype(bf16)
    kept = (slots < capacity) & live
    target = jnp.where(kept, expert_ids * cap_pad + slots, slot_total)
    place = (
        target[:, None, :] == jnp.arange(slot_total, dtype=jnp.int32)[None, :, None]
    ).astype(bf16)

    def to_slots(rows):
        moved = jnp.einsum("bcr,brd->bcd", place, rows, preferred_element_type=f32)
        moved = moved.astype(bf16).reshape(seqs, experts, cap_pad, width)
        return moved.transpose(1, 0, 2, 3).reshape(experts, seqs * cap_pad, width)

    def from_slots(rows):
        rows = rows.reshape(experts, seqs, cap_pad, width).transpose(1, 0, 2, 3)
        rows = rows.reshape(seqs, slot_total, width)
        return jnp.einsum("bcr,bcd->brd", place, rows, preferred_element_type=f32)

    slot_rows = seqs * cap_pad
    arrived = swap(jnp.concatenate([to_slots(normed2), to_slots(grad_picked)], axis=1), "ctx")
    rows_in = lax.all_gather(arrived[:, :slot_rows], "dp", axis=0, tiled=False)
    grads_in = lax.all_gather(arrived[:, slot_rows:], "dp", axis=0, tiled=False)
    rows_in = rows_in.reshape(-1, width)
    grads_in = grads_in.reshape(-1, width)

    expert_pre = dot(rows_in, win_part, 1, 0)
    expert_act = gelu_tanh(expert_pre).astype(bf16)
    produced = lax.psum_scatter(
        dot(expert_act, wout_part, 1, 0).astype(bf16), "dp", scatter_dimension=0, tiled=True
    )
    grad_act = dot(grads_in, wout_part, 1, 1)
    grad_pre = jax.vjp(gelu_tanh, expert_pre)[1](grad_act)[0].astype(bf16)
    grad_sent = lax.psum_scatter(
        dot(grad_pre, win_part, 1, 1).astype(bf16), "dp", scatter_dimension=0, tiled=True
    )
    grad_wout = dot(expert_act, grads_in, 0, 0)
    grad_win = dot(rows_in, grad_pre, 0, 0).astype(bf16)
    grad_win = swap(grad_win.reshape(dp_count, -1, ff_part), "dp").astype(f32)
    grad_win = grad_win.transpose(1, 0, 2).reshape(-1, FF)

    returned = swap(
        jnp.concatenate(
            [
                produced.reshape(ctx_count, slot_rows, width),
                grad_sent.reshape(ctx_count, slot_rows, width),
            ],
            axis=1,
        ),
        "ctx",
    )
    picked = from_slots(returned[:, :slot_rows])
    grad_expert_in = from_slots(returned[:, slot_rows:])
    output = (hidden + chosen[..., None] * picked).astype(bf16)

    grad_chosen = jnp.sum(grad_out * picked, axis=-1)
    grad_logits = gate_probs * (
        grad_chosen[..., None] * pick_mask - (grad_chosen * chosen)[..., None]
    )
    sum_router = jnp.einsum("bsd,bse->de", normed2.astype(f32), grad_logits, precision=precise)
    grad_normed2 = grad_expert_in + jnp.einsum(
        "bse,de->bsd", grad_logits, router_full.astype(f32), precision=precise
    )
    grad_hidden_norm, sum_gain_second = jax.vjp(rms_scale, hidden, gain_second)[1](grad_normed2)
    grad_hidden = grad_out + grad_hidden_norm
    grad_branch = grad_hidden.astype(bf16)
    grad_mixed = jnp.einsum(
        "bse,de->bds", grad_branch, out_full, preferred_element_type=f32
    ).astype(bf16)
    grad_mixed = jnp.pad(grad_mixed, ((0, 0), (0, all_cols - width), (0, 0)))
    grad_mixed = swap(grad_mixed.reshape(ctx_count, cols, block), "ctx")
    sum_out = jnp.einsum("bds,bse->de", mixed, grad_branch, preferred_element_type=f32)
    sum_out = lax.psum_scatter(sum_out.astype(bf16), "dp", scatter_dimension=0, tiled=True)

    grad_parts, diag = attend_back(
        projected, probs, grad_mixed.reshape(ctx_count, heads, DH, block)
    )
    grad_parts = grad_parts.reshape(3 * cols, length)
    normed_part = dot(grad_parts, w_heads, 0, 1).astype(bf16)
    normed_part = swap(normed_part.reshape(ctx_count, block, width), "ctx")
    grad_normed = jnp.sum(
        normed_part.reshape(seqs, groups, block, width).astype(f32), axis=1
    )
    sum_qkv = lax.psum_scatter(
        dot(normed_seq, grad_parts, 0, 1).astype(bf16), "dp", scatter_dimension=0, tiled=True
    )
    sum_out = swap(sum_out.reshape(ctx_count, own_rows, width), "ctx").astype(f32)
    grad_attn_out = jnp.sum(sum_out, axis=0)
    sum_qkv = swap(sum_qkv.reshape(ctx_count, own_rows, 3 * cols), "ctx").astype(f32)
    sum_qkv = jnp.sum(sum_qkv.reshape(seqs, groups, own_rows, 3, cols), axis=0)
    grad_attn_qkv = sum_qkv.transpose(2, 1, 0, 3).reshape(3, own_rows, all_cols)[..., :width]

    grad_x_norm, sum_gain_first = jax.vjp(rms_scale, x_float, gain_first)[1](grad_normed)
    grad_tokens = grad_hidden + grad_x_norm

    diag_line = sum(
        jnp.roll(diag[:, a, :], block - 1 - a, axis=1) for a in range(8)
    )
    sum_table = jnp.einsum(
        "wn,hw->nh", onehot_line.astype(f32), diag_line, precision=precise
    )
    sum_table = lax.dynamic_update_slice_in_dim(
        jnp.zeros((NB, groups * heads), f32), sum_table, my_group * heads, axis=1
    )[:, :H]
    table_col = pad_last(sum_table.reshape(-1, table_rows), own_rows).reshape(width, 1)
    sums = jnp.concatenate(
        [sum_gain_first[:, None], sum_gain_second[:, None], sum_router, table_col], axis=1
    )
    sums = swap(sums.reshape(dp_count * ctx_count, own_rows, -1), ("dp", "ctx"))
    sums = jnp.sum(sums, axis=0)
    return (
        output,
        grad_tokens,
        grad_attn_qkv,
        grad_attn_out,
        sums[:, :2].T,
        sums[:, 2 : 2 + experts],
        sums[:table_rows, 2 + experts],
        grad_win[None],
        grad_wout[None],
    )


def solution(mesh):
    in_specs = (
        P("dp", "ctx", None),
        P(None, ("dp", "ctx"), None),
        P(("dp", "ctx"), None),
        P(None, ("dp", "ctx")),
        P(("dp", "ctx"), None),
        P(("dp", "ctx")),
        P("ctx", "dp", None),
        P("ctx", "dp", None),
        P("dp", "ctx", None),
        P("dp", "ctx"),
        P(),
        P("dp", "ctx"),
        P("dp", "ctx"),
    )
    out_specs = (
        P("dp", "ctx", None),
        P("dp", "ctx", None),
        P(None, ("dp", "ctx"), None),
        P(("dp", "ctx"), None),
        P(None, ("dp", "ctx")),
        P(("dp", "ctx"), None),
        P(("dp", "ctx")),
        P("ctx", "dp", None),
        P("ctx", "dp", None),
    )
    return jax.shard_map(
        on_device, mesh=mesh, in_specs=in_specs, out_specs=out_specs, check_vma=False
    )
```
